256 devices in a mesh: dom: 64 (over x, z, core), mp: 4 (over y).
Axes of the slice: x: 4, y: 4, z: 8, core: 2. Of those that a mesh axis runs over, the one named last changes fastest.
Arguments:
- features: bfloat16 [262144, 512], P('dom', 'mp'), may hold values from -6 to 6
- history: bfloat16 [262144, 512], P('dom', 'mp'), may hold values from -6 to 6
- weight: bfloat16 [512, 512], P(None, 'mp'), may hold values from -0.25 to 0.25
- bias_vector: float32 [512], P('mp'), may hold values from -3 to 3
- cotangent: bfloat16 [262144, 512], P('dom', 'mp'), may hold values from -6 to 6
- adj_tiles: bfloat16 [12288, 128, 128], P('dom'), may hold values from 0 to 0.071777344
- send_list: int32 [64, 64, 2], P('dom'), may hold values from -1 to 63, as said below
- batch_slot: int32 [64, 32], P('dom'), may hold values from 0 to 126, as said below
- tile_src: int32 [64, 192], P('dom'), may hold values from 0 to 127, as said below
Outputs:
- refreshed: bfloat16 [262144, 512], P('dom', 'mp')
- feat_grad: bfloat16 [262144, 512], P('dom', 'mp')
- weight_grad: float32 [512, 512], P(None, 'mp')
- bias_grad: float32 [512], P('mp')
The draws below stay inside these ranges and needn't reach their ends.
Inputs may be any that keep to these rules, and one draw needn't show every extreme that they name: send_list[s, c, k] names a block of owner s's table (feature blocks 0..31, then history blocks 32..63) or is -1 for an empty slot. Feature block j of each owner stands in exactly one entry over all c, always in slot 0; slot 1 never holds a feature block. batch_slot[c, j] = s * 2 + j // 64 for the one owner s with send_list[s, c, j // 64] = j. tile_src[c, t] is a slot s * 2 + k with send_list[s, c, k] >= 0; tile t of device c feeds batch block t // 6.
All inputs are finite; a program needn't handle non-finite values.
Results may differ from the reference program's by a relative error of at most 0.012.
Values may be sent and summed in bfloat16 or wider, within the bound.
A program may use at most 128 MiB of HBM per device.

```python
import jax
import jax.numpy as jnp
from jax import lax

HID = 512
BLK = 128
BLOCKS = 32
TPR = 6
SLOTS = 2
ALL_TILES = 12288
NODES = 262144
N_DOM = 64


def routing(key):
    order = jax.random.permutation(jax.random.fold_in(key, 11), N_DOM)
    inverse = jnp.argsort(order)
    lane_count = SLOTS - 1
    offsets = jnp.concatenate([jax.random.permutation(jax.random.fold_in(key, 20 + lane), N_DOM) for lane in range(lane_count)])[:BLOCKS]
    devices = jnp.arange(N_DOM)
    owner_of = inverse[(order[:, None] + offsets[None, :]) % N_DOM]
    lane_of = jnp.arange(BLOCKS) // N_DOM
    slot_of = owner_of * SLOTS + lane_of[None, :]
    batch_fill = jnp.full((N_DOM, N_DOM * SLOTS), -1, jnp.int32)
    batch_fill = batch_fill.at[devices[:, None], slot_of].set(jnp.broadcast_to(jnp.arange(BLOCKS)[None, :], (N_DOM, BLOCKS)).astype(jnp.int32))
    coin = jax.random.randint(jax.random.fold_in(key, 12), (N_DOM, N_DOM * SLOTS), 0, 2)
    pick = jax.random.randint(jax.random.fold_in(key, 13), (N_DOM, N_DOM * SLOTS), BLOCKS, 2 * BLOCKS)
    halo_fill = jnp.where(coin == 1, pick, -1)
    forced = owner_of[:, 0] * SLOTS + SLOTS - 1
    halo_fill = halo_fill.at[devices, forced].set(pick[devices, forced])
    merged = jnp.where(batch_fill >= 0, batch_fill, halo_fill)
    return (merged.astype(jnp.int32), slot_of.astype(jnp.int32))


def draw_send_list(key, part):
    merged, slot_of = routing(key)
    return merged.reshape(N_DOM, N_DOM, SLOTS).transpose(1, 0, 2).astype(jnp.int32)


def draw_batch_slot(key, part):
    merged, slot_of = routing(key)
    return slot_of.astype(jnp.int32)


def draw_tile_src(key, part):
    merged, slot_of = routing(key)
    key = jax.random.fold_in(key, 3)
    live = merged >= 0
    width_all = N_DOM * SLOTS
    scores = jax.random.randint(key, (N_DOM, BLOCKS, width_all), 0, 2 ** 20) * width_all + jnp.arange(width_all)[None, None, :]
    masked = jnp.where(live[:, None, :], scores, -1).astype(jnp.int32)
    values, indices = lax.top_k(masked, TPR - 1)
    chosen = jnp.where(values >= 0, indices.astype(jnp.int32), slot_of[:, :, None])
    tiles_all = jnp.concatenate([slot_of[:, :, None], chosen], axis=2)
    return tiles_all.reshape(N_DOM, BLOCKS * TPR).astype(jnp.int32)


def steps_of(stream_key, shape, pieces, least, top_value):
    factor_of, own = 1.0, jax.random.fold_in(stream_key, 6)
    for position, parts in pieces:
        steps = jnp.exp(jax.random.uniform(jax.random.fold_in(own, position), (parts,), jnp.float32, least / len(pieces), top_value / len(pieces)))
        factor_of = factor_of * jnp.repeat(steps, shape[position] // parts).reshape([-1 if axis == position else 1 for axis in range(len(shape))])
    return factor_of


def centred(own_key, shape, spread, most, cuts=(), dtype=jnp.bfloat16):
    gain = steps_of(own_key, shape, cuts, -0.22, 0.18) if cuts else 1.0
    entries = jax.random.normal(own_key, shape, jnp.float32) * spread * gain
    return jnp.minimum(jnp.maximum(entries, -most), most).astype(dtype)


def setup_inputs(seed: int = 0) -> dict:
    arg_keys = jax.random.split(jax.random.key(seed), 10)
    features = centred(arg_keys[0], (NODES, HID), 1.0, 6.0, ((0, 64), (1, 4)))
    history = centred(arg_keys[1], (NODES, HID), 1.0, 6.0, ((0, 64), (1, 4)))
    weight = centred(arg_keys[2], (HID, HID), HID ** -0.5, 0.25, ((1, 4),))
    bias_vector = centred(arg_keys[3], (HID,), 0.5, 3.0, ((0, 4),), jnp.float32)
    cotangent = centred(arg_keys[4], (NODES, HID), 1.0, 6.0, ((0, 64), (1, 4)))
    adj_tiles = jnp.clip(0.071777344 * jax.random.uniform(arg_keys[5], (ALL_TILES, BLK, BLK), jnp.float32) ** steps_of(arg_keys[5], (ALL_TILES, BLK, BLK), ((0, 64),), -0.2, 0.2), 0.0, 0.071777344).astype(jnp.bfloat16)
    send_list = draw_send_list(jax.random.fold_in(arg_keys[9], 71), 0)
    batch_slot = draw_batch_slot(jax.random.fold_in(arg_keys[9], 71), 0)
    tile_src = draw_tile_src(jax.random.fold_in(arg_keys[9], 71), 0)
    return {"features": features, "history": history, "weight": weight, "bias_vector": bias_vector, "cotangent": cotangent, "adj_tiles": adj_tiles, "send_list": send_list, "batch_slot": batch_slot, "tile_src": tile_src}


def activate(preact):
    return jax.nn.gelu(preact, approximate=True)

def reference(features, history, weight, bias_vector, cotangent, adj_tiles, send_list, batch_slot, tile_src):
    feat_blocks = features.reshape(N_DOM, BLOCKS, BLK, HID)
    hist_blocks = history.reshape(N_DOM, BLOCKS, BLK, HID)
    own_table = jnp.concatenate([feat_blocks, hist_blocks], axis=1)
    tile_blocks = adj_tiles.reshape(N_DOM, BLOCKS, TPR, BLK, BLK)
    cot_blocks = cotangent.reshape(N_DOM, BLOCKS * BLK, HID)
    owners = jnp.arange(N_DOM).astype(jnp.int32)[:, None]

    def one_batch(device):
        wanted = send_list[:, device, :]
        picked = own_table[owners, jnp.clip(wanted, 0, 2 * BLOCKS - 1).astype(jnp.int32)]
        slot_data = jnp.where(wanted[:, :, None, None] >= 0, picked, jnp.zeros_like(picked))
        slot_data = slot_data.reshape(N_DOM * SLOTS, BLK, HID)
        sources = slot_data[tile_src[device]].reshape(BLOCKS, TPR, BLK, HID)
        tiles_here = tile_blocks[device].astype(jnp.float32)
        mixed = jnp.einsum('jpab,jpbh->jah', tiles_here, sources.astype(jnp.float32)).astype(jnp.bfloat16)
        mixed_rows = mixed.reshape(BLOCKS * BLK, HID)
        preact = jnp.dot(mixed_rows, weight, preferred_element_type=jnp.float32) + bias_vector
        fresh_rows, pullback = jax.vjp(activate, preact)
        pre_grad = pullback(cot_blocks[device].astype(jnp.float32))[0].astype(jnp.bfloat16)
        weight_part = jnp.dot(mixed_rows.T, pre_grad, preferred_element_type=jnp.float32)
        bias_part = lax.optimization_barrier(jnp.sum(pre_grad.astype(jnp.float32), axis=0))
        agg_grad = jnp.dot(pre_grad, weight.T, preferred_element_type=jnp.float32).astype(jnp.bfloat16)
        agg_grad = agg_grad.reshape(BLOCKS, BLK, HID).astype(jnp.float32)
        back_terms = jnp.einsum('jpab,jah->jpbh', tiles_here, agg_grad).reshape(BLOCKS * TPR, BLK, HID)
        hit_table = (tile_src[device][:, None] == batch_slot[device][None, :]).astype(jnp.float32)
        block_grad = jnp.einsum('tj,tbh->jbh', hit_table, back_terms).astype(jnp.bfloat16)
        fresh_blocks = fresh_rows.astype(jnp.bfloat16).reshape(BLOCKS, BLK, HID)
        return (fresh_blocks, block_grad, weight_part, bias_part)
    fresh_all, grad_all, weight_parts, bias_parts = lax.map(one_batch, jnp.arange(N_DOM).astype(jnp.int32))
    owner_rank = (batch_slot // SLOTS).astype(jnp.int32)
    block_ids = jnp.broadcast_to(jnp.arange(BLOCKS).astype(jnp.int32)[None, :], (N_DOM, BLOCKS))
    empty = jnp.zeros((N_DOM, BLOCKS, BLK, HID), jnp.bfloat16)
    refreshed = empty.at[owner_rank, block_ids].set(fresh_all).reshape(NODES, HID)
    feat_grad = empty.at[owner_rank, block_ids].set(grad_all).reshape(NODES, HID)
    weight_grad = lax.optimization_barrier(jnp.sum(weight_parts, axis=0)) / N_DOM
    bias_grad = lax.optimization_barrier(jnp.sum(bias_parts, axis=0)) / N_DOM
    return (refreshed, feat_grad, weight_grad, bias_grad)
```

```python
import functools
import math

import jax
import jax.numpy as jnp
from jax import lax
from jax.experimental import pallas as pl
from jax.experimental.pallas import tpu as pltpu
from jax.sharding import PartitionSpec as P

MESH = pl.DeviceIdType.MESH
CHUNKS = 2
BF16 = jnp.bfloat16
F32 = jnp.float32


def drain(ref, sem):
    pltpu.make_async_copy(ref, ref, sem).wait()


def layer_kernel(
    dims,
    idx,
    bias,
    feat,
    hist,
    weight,
    cot,
    adj,
    fresh_out,
    grad_out,
    wgrad_out,
    bgrad_out,
    tab,
    stage,
    arr,
    adj_v,
    adj_t,
    cotx,
    wx,
    w_full,
    w_t,
    bias_st,
    biasx,
    mixed,
    mixx,
    pg,
    fst,
    fx,
    ast,
    ax,
    rarr,
    cum,
    garr,
    wp,
    wpx,
    ws,
    rsb,
    bsb,
    fin,
    bfin,
    wfin,
    bres,
    loc,
    ysend,
    yrecv,
    zsend,
    zrecv,
):
    n_dom, n_mp, blocks, tpr, blk, col, off = dims
    group = blocks // n_mp
    rows_q = blk // CHUNKS
    tiles = blocks * tpr
    dom = lax.axis_index("dom")
    mp = lax.axis_index("mp")

    def dom_at(i):
        return lax.rem(dom + i, n_dom)

    def mp_at(i):
        return lax.rem(mp + i, n_mp)

    def push(src, dst, send, recv, where):
        pltpu.make_async_remote_copy(
            src_ref=src,
            dst_ref=dst,
            send_sem=send,
            recv_sem=recv,
            device_id=where,
            device_id_type=MESH,
        ).start()

    def over_dom(body):
        lax.fori_loop(1, n_dom, lambda i, c: (body(i), c)[1], 0)

    barrier = pltpu.get_barrier_semaphore()
    for r in range(1, n_mp):
        pl.semaphore_signal(barrier, inc=1, device_id=(dom, mp_at(r)), device_id_type=MESH)
    over_dom(
        lambda i: pl.semaphore_signal(
            barrier, inc=1, device_id=(dom_at(i), mp), device_id_type=MESH
        )
    )
    load_feat = pltpu.make_async_copy(feat, tab.at[pl.ds(0, blocks)], loc.at[0])
    load_hist = pltpu.make_async_copy(hist, tab.at[pl.ds(blocks, blocks)], loc.at[1])
    load_adj = pltpu.make_async_copy(adj, adj_v, loc.at[2])
    own_group = pl.ds(pl.multiple_of(mp * group, group), group)
    load_cot = pltpu.make_async_copy(cot.at[own_group], cotx.at[mp], loc.at[3])
    load_w = pltpu.make_async_copy(weight, wx.at[mp], loc.at[4])
    load_feat.start()
    load_hist.start()
    load_w.start()
    load_cot.start()
    load_adj.start()
    bias_st[...] = jnp.broadcast_to(bias[...], bias_st.shape)
    biasx[mp] = bias_st[...]
    load_feat.wait()
    load_hist.wait()
    pl.semaphore_wait(barrier, n_dom - 1 + n_mp - 1)

    def table_block(d, k):
        return tab[jnp.maximum(idx[off["send"] + 2 * d + k], 0)]

    def send_slots(i):
        d = dom_at(i)
        stage[2 * i] = table_block(d, 0)
        stage[2 * i + 1] = table_block(d, 1)
        push(
            stage.at[pl.ds(2 * i, 2)],
            arr.at[pl.ds(2 * dom, 2)],
            zsend.at[0],
            zrecv.at[0],
            (d, mp),
        )

    over_dom(send_slots)
    arr[2 * dom] = table_block(dom, 0)
    arr[2 * dom + 1] = table_block(dom, 1)

    for r in range(1, n_mp):
        g = mp_at(r)
        theirs = pl.ds(pl.multiple_of(g * group, group), group)
        push(weight, wx.at[mp], ysend.at[0], yrecv.at[0], (dom, g))
        push(bias_st, biasx.at[mp], ysend.at[1], yrecv.at[1], (dom, g))
        push(cot.at[theirs], cotx.at[mp], ysend.at[2], yrecv.at[2], (dom, g))

    load_adj.wait()

    def flip(t, c):
        adj_t[t] = adj_v[t].T
        return c

    lax.fori_loop(0, tiles, flip, 0, unroll=4)

    load_w.wait()
    drain(wx.at[pl.ds(0, n_mp - 1)], yrecv.at[0])
    for m in range(n_mp):
        w_full[:, m * col : (m + 1) * col] = wx[m]
        w_t[m * col : (m + 1) * col, :] = wx[m].T
    drain(biasx.at[pl.ds(0, n_mp - 1)], yrecv.at[1])
    load_cot.wait()
    drain(cotx.at[pl.ds(0, n_mp - 1)], yrecv.at[2])
    bias_row = jnp.concatenate([biasx[m][0:1] for m in range(n_mp)], axis=1)

    drain(stage.at[pl.ds(0, 2 * (n_dom - 1))], zrecv.at[0])

    def mix(q):
        for r in list(range(1, n_mp)) + [0]:
            g = mp_at(r)

            def one(jj, c):
                j = g * group + jj
                left = jnp.concatenate(
                    [adj_v[j * tpr + p, q * rows_q : (q + 1) * rows_q, :] for p in range(tpr)],
                    axis=1,
                )
                right = jnp.concatenate(
                    [arr[idx[off["src"] + j * tpr + p]] for p in range(tpr)], axis=0
                )
                out = jnp.dot(left, right, preferred_element_type=F32).astype(BF16)
                if r:
                    mixed[q, j] = out
                else:
                    mixx[q, mp, jj] = out
                return c

            lax.fori_loop(0, group, one, 0, unroll=2)
            if r:
                theirs = pl.ds(pl.multiple_of(g * group, group), group)
                push(
                    mixed.at[q, theirs],
                    mixx.at[q, mp],
                    ysend.at[3 + q],
                    yrecv.at[3 + q],
                    (dom, g),
                )

    per = 2
    hid = n_mp * col
    root = math.sqrt(2.0 / math.pi)

    def dense(q):
        def one(s, bias_acc):
            b0 = pl.multiple_of(s * per, per)
            x = jnp.concatenate(
                [mixx[q, m, pl.ds(b0, per)].reshape(per * rows_q, col) for m in range(n_mp)],
                axis=1,
            )
            v = jnp.dot(x, w_full[...], preferred_element_type=F32) + bias_row
            square = v * v
            t = jnp.tanh(root * v * (1.0 + 0.044715 * square))
            half = 0.5 * (1.0 + t)
            fresh = (v * half).astype(BF16)
            slope = half + 0.5 * v * (1.0 - t * t) * (root * (1.0 + 3 * 0.044715 * square))
            c = jnp.concatenate(
                [
                    cotx[m, pl.ds(b0, per), q * rows_q : (q + 1) * rows_q, :].reshape(
                        per * rows_q, col
                    )
                    for m in range(n_mp)
                ],
                axis=1,
            )
            p = (c.astype(F32) * slope).astype(BF16)
            pg[q, pl.ds(pl.multiple_of(s * per * rows_q, per * rows_q), per * rows_q), :] = p
            agg = jnp.dot(p, w_t[...], preferred_element_type=F32).astype(BF16)
            for m in range(n_mp):
                cut = slice(m * col, (m + 1) * col)
                fst[q, m, pl.ds(b0, per)] = fresh[:, cut].reshape(per, rows_q, col)
                ast[q, m, pl.ds(b0, per)] = agg[:, cut].reshape(per, rows_q, col)
            return bias_acc + jnp.sum(p.astype(F32).reshape(-1, 8, hid), axis=0)

        total = lax.fori_loop(0, group // per, one, jnp.zeros((8, hid), F32))
        pltpu.make_async_copy(fst.at[q, mp], fx[q].at[own_group], loc.at[5 + q]).start()
        pltpu.make_async_copy(ast.at[q, mp], ax.at[q, own_group], loc.at[5 + CHUNKS + q]).start()
        for r in range(1, n_mp):
            g = mp_at(r)
            push(
                fst.at[q, g],
                fx[q].at[own_group],
                ysend.at[3 + CHUNKS + q],
                yrecv.at[3 + CHUNKS + q],
                (dom, g),
            )
        for r in range(1, n_mp):
            g = mp_at(r)
            push(
                ast.at[q, g],
                ax.at[q, own_group],
                ysend.at[3 + 2 * CHUNKS + q],
                yrecv.at[3 + 2 * CHUNKS + q],
                (dom, g),
            )
        return total

    drain(stage.at[pl.ds(0, 2 * (n_dom - 1))], zsend.at[0])

    def return_fresh(q):
        pltpu.make_async_copy(fst.at[q, mp], fx[q].at[own_group], loc.at[5 + q]).wait()
        drain(fst.at[q, pl.ds(0, n_mp - 1)], yrecv.at[3 + CHUNKS + q])

        def one(i):
            d = dom_at(i)
            stage[i, q * rows_q : (q + 1) * rows_q, :] = fx[q][idx[off["inv"] + d]]
            push(
                stage.at[i, pl.ds(q * rows_q, rows_q)],
                rarr[q].at[dom],
                zsend.at[1 + q],
                zrecv.at[1 + q],
                (d, mp),
            )

        over_dom(one)
        rarr[q][dom] = fx[q][idx[off["inv"] + dom]]

    mix(0)
    bias_acc = jnp.zeros((8, hid), F32)
    for q in range(CHUNKS):
        if q + 1 < CHUNKS:
            mix(q + 1)
        drain(mixx.at[q, pl.ds(0, n_mp - 1)], yrecv.at[3 + q])
        bias_acc = bias_acc + dense(q)
        if q >= 1:
            return_fresh(q - 1)
    return_fresh(CHUNKS - 1)

    for m in range(n_mp):
        part = jnp.zeros((col, hid), F32)
        for q in range(CHUNKS):
            part = part + lax.dot_general(
                mixx[q, m].reshape(group * rows_q, col),
                pg[q],
                (((0,), (0,)), ((), ())),
                preferred_element_type=F32,
            )
        for m2 in range(n_mp):
            wp[m2, m * (col // 8) : (m + 1) * (col // 8)] = part[
                :, m2 * col : (m2 + 1) * col
            ].reshape(col // 8, 8, col)
    for m in range(n_mp):
        wp[m, hid // 8] = bias_acc[:, m * col : (m + 1) * col]
    for r in range(1, n_mp):
        g = mp_at(r)
        push(wp.at[g], wpx.at[mp], ysend.at[3 + 3 * CHUNKS], yrecv.at[3 + 3 * CHUNKS], (dom, g))
    wpx[mp] = wp[mp]

    for q in range(CHUNKS):
        pltpu.make_async_copy(
            ast.at[q, mp], ax.at[q, own_group], loc.at[5 + CHUNKS + q]
        ).wait()
        drain(ast.at[q, pl.ds(0, n_mp - 1)], yrecv.at[3 + 2 * CHUNKS + q])

    step = 8

    def back(s, acc):
        terms = []
        for u in range(step):
            i = s * step + u
            t = idx[off["order"] + i]
            b = idx[off["block"] + i]
            rows = jnp.concatenate([ax[q, b] for q in range(CHUNKS)], axis=0)
            terms.append(jnp.dot(adj_t[t], rows, preferred_element_type=F32))
        for u in range(step):
            i = s * step + u
            acc = jnp.where(idx[off["new"] + i] > 0, terms[u], acc + terms[u])
            cum[i] = acc.astype(BF16)
        return acc

    lax.fori_loop(0, tiles // step, back, jnp.zeros((blk, col), F32))

    drain(wp.at[pl.ds(0, n_mp - 1)], yrecv.at[3 + 3 * CHUNKS])
    chunks = hid // 8
    total = wpx[0]
    for m in range(1, n_mp):
        total = total + wpx[m]
    ws[...] = total

    def send_rows(i):
        d = dom_at(i)
        push(ws.at[d], rsb.at[dom], zsend.at[1 + CHUNKS], zrecv.at[1 + CHUNKS], (d, mp))

    over_dom(send_rows)
    rsb[dom] = ws[dom]

    @pl.when(dom != 0)
    def _():
        push(ws.at[chunks], bsb.at[dom], zsend.at[2 + CHUNKS], zrecv.at[2 + CHUNKS], (0, mp))

    def grad_block(d):
        at = idx[off["end"] + d]
        found = cum[jnp.maximum(at, 0)]
        return jnp.where(at >= 0, found, jnp.zeros_like(found))

    def send_grad(i):
        d = dom_at(i)
        stage[n_dom + i] = grad_block(d)
        push(stage.at[n_dom + i], garr.at[dom], zsend.at[3 + CHUNKS], zrecv.at[3 + CHUNKS], (d, mp))

    over_dom(send_grad)
    garr[dom] = grad_block(dom)

    drain(rsb.at[pl.ds(0, n_dom - 1)], zrecv.at[1 + CHUNKS])
    fin[...] = jnp.sum(rsb[...], axis=0) * (1.0 / n_dom)
    over_dom(
        lambda i: push(fin, wfin.at[dom], zsend.at[4 + CHUNKS], zrecv.at[4 + CHUNKS], (dom_at(i), mp))
    )
    wfin[dom] = fin[...]

    @pl.when(dom == 0)
    def _():
        bsb[0] = ws[chunks]
        drain(bsb.at[pl.ds(0, n_dom - 1)], zrecv.at[2 + CHUNKS])
        line = jnp.sum(jnp.sum(bsb[...], axis=0), axis=0, keepdims=True) * (1.0 / n_dom)
        bfin[...] = jnp.broadcast_to(line, bfin.shape)
        over_dom(
            lambda i: push(bfin, bres, zsend.at[5 + CHUNKS], zrecv.at[5 + CHUNKS], (dom_at(i), mp))
        )
        bgrad_out[...] = line

    for q in range(CHUNKS):
        drain(rarr[q].at[pl.ds(0, n_dom - 1)], zrecv.at[1 + q])

        def settle(j, c):
            fresh_out[j, q * rows_q : (q + 1) * rows_q, :] = rarr[q][idx[off["rev"] + j]]
            return c

        lax.fori_loop(0, blocks, settle, 0, unroll=2)

    @pl.when(dom != 0)
    def _():
        drain(bres, zrecv.at[5 + CHUNKS])
        bgrad_out[...] = bres[0:1]

    drain(wfin.at[pl.ds(0, n_dom - 1)], zrecv.at[4 + CHUNKS])
    wgrad_out[...] = wfin[...]
    drain(garr.at[pl.ds(0, n_dom - 1)], zrecv.at[3 + CHUNKS])

    def settle_grad(j, c):
        grad_out[j] = garr[idx[off["rev"] + j]]
        return c

    lax.fori_loop(0, blocks, settle_grad, 0, unroll=2)

    peers = pl.ds(0, n_mp - 1)
    others = pl.ds(0, n_dom - 1)
    drain(wx.at[peers], ysend.at[0])
    drain(biasx.at[peers], ysend.at[1])
    drain(cotx.at[peers], ysend.at[2])
    for q in range(CHUNKS):
        drain(mixx.at[q, peers], ysend.at[3 + q])
        drain(fst.at[q, peers], ysend.at[3 + CHUNKS + q])
        drain(ast.at[q, peers], ysend.at[3 + 2 * CHUNKS + q])
        drain(rarr[q].at[others], zsend.at[1 + q])
    drain(wp.at[peers], ysend.at[3 + 3 * CHUNKS])
    drain(rsb.at[others], zsend.at[1 + CHUNKS])
    drain(garr.at[others], zsend.at[3 + CHUNKS])
    drain(wfin.at[others], zsend.at[4 + CHUNKS])

    @pl.when(dom != 0)
    def _():
        drain(ws.at[chunks], zsend.at[2 + CHUNKS])

    @pl.when(dom == 0)
    def _():
        drain(bsb.at[others], zsend.at[5 + CHUNKS])


def on_device(
    features, history, weight, bias_vector, cotangent, adj_tiles, send_list, batch_slot, tile_src
):
    n_dom = lax.axis_size("dom")
    n_mp = lax.axis_size("mp")
    blk = adj_tiles.shape[1]
    col = features.shape[1]
    blocks = features.shape[0] // blk
    tiles = tile_src.shape[1]
    tpr = tiles // blocks
    hid = n_mp * col
    group = blocks // n_mp
    rows_q = blk // CHUNKS

    wanted = send_list[0]
    slots = batch_slot[0]
    src = tile_src[0]
    ids = jnp.arange(blocks, dtype=jnp.int32)
    doms = jnp.arange(n_dom, dtype=jnp.int32)
    ts = jnp.arange(tiles, dtype=jnp.int32)
    owner = slots // 2
    inverse = jnp.sum(jnp.where(owner[None, :] == doms[:, None], ids[None, :], 0), axis=1)
    reverse = jnp.sum(jnp.where(wanted[:, 0][None, :] == ids[:, None], doms[None, :], 0), axis=1)
    hit = src[:, None] == slots[None, :]
    target = blocks - jnp.sum(jnp.where(hit, blocks - ids[None, :], 0), axis=1)
    key = target * tiles + ts
    rank = jnp.sum((key[None, :] < key[:, None]).astype(jnp.int32), axis=1)
    place = rank[None, :] == ts[:, None]
    order = jnp.sum(jnp.where(place, ts[None, :], 0), axis=1)
    count = jnp.sum(hit.astype(jnp.int32), axis=0)
    upto = jnp.sum((target[:, None] <= ids[None, :]).astype(jnp.int32), axis=0)
    begin = upto - count
    new = jnp.sum(
        jnp.where((begin[None, :] == ts[:, None]) & (count > 0)[None, :], 1, 0), axis=1
    ) + (ts == upto[-1])
    last = jnp.where(count > 0, upto - 1, -1)
    last_of = jnp.sum(
        jnp.where(owner[None, :] == doms[:, None], last[None, :] + 1, 0), axis=1
    ) - 1
    pieces = [
        ("send", wanted.reshape(-1)),
        ("src", src),
        ("inv", inverse),
        ("rev", reverse),
        ("order", order),
        ("block", order // tpr),
        ("new", new),
        ("end", last_of),
    ]
    off, at = {}, 0
    for name, piece in pieces:
        off[name] = at
        at += piece.shape[0]
    idx = jnp.concatenate([piece.astype(jnp.int32) for _, piece in pieces])

    vm = pltpu.VMEM
    scratch = [
        vm((2 * blocks, blk, col), BF16),
        vm((2 * n_dom, blk, col), BF16),
        vm((2 * n_dom, blk, col), BF16),
        vm((tiles, blk, blk), BF16),
        vm((tiles, blk, blk), BF16),
        vm((n_mp, group, blk, col), BF16),
        vm((n_mp, hid, col), BF16),
        vm((hid, hid), BF16),
        vm((hid, hid), BF16),
        vm((8, col), F32),
        vm((n_mp, 8, col), F32),
        vm((CHUNKS, blocks, rows_q, col), BF16),
        vm((CHUNKS, n_mp, group, rows_q, col), BF16),
        vm((CHUNKS, group * rows_q, hid), BF16),
        vm((CHUNKS, n_mp, group, rows_q, col), BF16),
        tuple(vm((blocks, rows_q, col), BF16) for _ in range(CHUNKS)),
        vm((CHUNKS, n_mp, group, rows_q, col), BF16),
        vm((CHUNKS, blocks, rows_q, col), BF16),
        tuple(vm((n_dom, rows_q, col), BF16) for _ in range(CHUNKS)),
        vm((tiles, blk, col), BF16),
        vm((n_dom, blk, col), BF16),
        vm((n_mp, hid // 8 + 1, 8, col), F32),
        vm((n_mp, hid // 8 + 1, 8, col), F32),
        vm((hid // 8 + 1, 8, col), F32),
        vm((n_dom, 8, col), F32),
        vm((n_dom, 8, col), F32),
        vm((8, col), F32),
        vm((8, col), F32),
        vm((n_dom, 8, col), F32),
        vm((8, col), F32),
        pltpu.SemaphoreType.DMA((5 + 2 * CHUNKS,)),
        pltpu.SemaphoreType.DMA((4 + 3 * CHUNKS,)),
        pltpu.SemaphoreType.DMA((4 + 3 * CHUNKS,)),
        pltpu.SemaphoreType.DMA((6 + CHUNKS,)),
        pltpu.SemaphoreType.DMA((6 + CHUNKS,)),
    ]
    in_vmem = pl.BlockSpec(memory_space=pltpu.VMEM)
    anywhere = pl.BlockSpec(memory_space=pl.ANY)
    dims = (n_dom, n_mp, blocks, tpr, blk, col, off)
    fresh, grad, wgrad, bgrad = pl.pallas_call(
        functools.partial(layer_kernel, dims),
        name="layer",
        out_shape=(
            jax.ShapeDtypeStruct((blocks, blk, col), BF16),
            jax.ShapeDtypeStruct((blocks, blk, col), BF16),
            jax.ShapeDtypeStruct((n_dom, 8, col), F32),
            jax.ShapeDtypeStruct((1, col), F32),
        ),
        in_specs=[pl.BlockSpec(memory_space=pltpu.SMEM), in_vmem] + [anywhere] * 5,
        out_specs=(in_vmem,) * 4,
        scratch_shapes=scratch,
        compiler_params=pltpu.CompilerParams(
            collective_id=1, has_side_effects=True, vmem_limit_bytes=60 * 1024 * 1024
        ),
    )(
        idx,
        bias_vector.reshape(1, col),
        features.reshape(blocks, blk, col),
        history.reshape(blocks, blk, col),
        weight,
        cotangent.reshape(blocks, blk, col),
        adj_tiles,
    )
    return (
        fresh.reshape(blocks * blk, col),
        grad.reshape(blocks * blk, col),
        wgrad.reshape(hid, col),
        bgrad.reshape(col),
    )


def solution(mesh):
    placed = (
        P("dom", "mp"),
        P("dom", "mp"),
        P(None, "mp"),
        P("mp"),
        P("dom", "mp"),
        P("dom", None, None),
        P("dom", None, None),
        P("dom", None),
        P("dom", None),
    )
    return jax.shard_map(
        on_device,
        mesh=mesh,
        in_specs=placed,
        out_specs=(P("dom", "mp"), P("dom", "mp"), P(None, "mp"), P("mp")),
        check_vma=False,
    )
```
